32 devices in a mesh: groups: 2 (over y), expert: 4 (over z), dp: 4 (over x, core).
Axes of the slice: x: 2, y: 2, z: 4, core: 2. Of those that a mesh axis runs over, the one named last changes fastest.
Arguments:
- tokens: bfloat16 [4096, 7168], P(('groups', 'expert', 'dp')), parts along dimension 0, may hold values from -6 to 6
- expert_ids: int32 [4096, 8], P(('groups', 'expert', 'dp')), parts along dimension 0, may hold values from 0 to 255, all different within a row; in each aligned block of 128 rows (0 to 127, 128 to 255, ...) at most 8 rows name the same one
Outputs:
- routed_hessian: float32 [8, 384, 7168], P(('groups', 'expert'), None, 'dp'), parts along dimension 0
- shared_hessian: float32 [14336, 128], P(('groups', 'expert', 'dp')), parts along dimension 0
The draws below stay inside these ranges and needn't reach their ends.
There are 2 independent parts, one for each index of `groups`. The reference program is written for one: setup_inputs(seed, part) draws one part's arguments, and reference() takes and returns one part's arrays. A program takes and returns all parts, laid end to end along the dimension named above; each array names one. Nothing has to cross between parts.
Inputs may be any that keep to these rules, and one draw needn't show every extreme that they name: `expert_ids`: each row names 8 different experts; within the rows of one device no expert is named by more than 8 rows; every expert is named by some row.
All inputs are finite; a program needn't handle non-finite values.
Results may differ from the reference program's by a relative error of at most 0.0003.
Values may be sent and summed in bfloat16 or wider, within the bound.
No kernel may reach another device: no remote copies, remote signals or barrier semaphores. Data moves between devices by JAX's collectives and lax.ppermute only.
A program may use at most 128 MiB of HBM per device.

```python
import math
import jax
import jax.numpy as jnp
import numpy as np
from jax import lax

D = 7168
E_ALL = 256
TOP = 8
TOK_DEV = 128
BAND = 384
SBAND = 128
CAP = 8
WINDOW = 4
TOKENS = 2048
N_EXPERT = 4
N_DP = 4


def strengthened(values, key, source, target, blocks, factor):
    def block_of(position):
        return (jnp.arange(values.shape[position]) // (values.shape[position] // blocks)).reshape((-1,) + (1,) * (values.ndim - 1 - position))

    one_side = jax.random.permutation(key, blocks)[block_of(target)]
    second = (block_of(target) + blocks // 2) % blocks
    return jnp.where((block_of(source) == one_side) | (block_of(source) == second), factor * values, values)


def level_of(stream_key, shape, shards, least, top_value):
    factor_of, own = 1.0, jax.random.fold_in(stream_key, 6)
    for position, shards_of in shards:
        steps = jnp.exp(jax.random.uniform(jax.random.fold_in(own, position), (shards_of,), jnp.float32, least / len(shards), top_value / len(shards)))
        factor_of = factor_of * jnp.repeat(steps, shape[position] // shards_of).reshape([-1 if axis == position else 1 for axis in range(len(shape))])
    return factor_of


def assign_block(own_key, own, number, rows, number_of, top, reach, slope):
    sequence = jax.random.permutation(own_key, number_of)
    packed, usual = shares(number_of, rows * top, reach, slope, True), shares(number_of, rows * top, reach, slope, False)
    places = jnp.arange(number_of)

    def named(lengths, turn):
        used = int((lengths > 0).sum())
        fixed = max(1, used // 4)
        shifted = fixed + (places - fixed + turn * (used - fixed)) % max(1, number_of - fixed)
        return jnp.zeros((number_of,), jnp.int32).at[sequence[jnp.where(places < fixed, places, shifted)]].set(jnp.asarray(lengths, jnp.int32))

    lengths = jnp.where(number % 4 == 0, named(packed, number // 4), named(usual, number - number // 4 - 1))
    mixed = jax.random.permutation(jax.random.fold_in(own, 3), number_of)
    donor, taker = mixed[0:number_of // 2 * 2:2], mixed[1:number_of // 2 * 2:2]
    room = jnp.minimum(lengths[donor] - 1, reach - lengths[taker]) // 2
    room = jnp.where((donor == sequence[0]) | (taker == sequence[0]) | (lengths[taker] == 0), 0, jnp.maximum(room, 0))
    shifted = jax.random.randint(jax.random.fold_in(own, 4), (number_of // 2,), 0, 1 << 20) % (room + 1)
    lengths = lengths.at[donor].add(-shifted).at[taker].add(shifted)
    labels = jnp.searchsorted(jnp.cumsum(lengths), jnp.arange(rows * top), side="right").astype(jnp.int32)
    table = labels.reshape(top, rows).T
    table = table[jax.random.permutation(jax.random.fold_in(own, 1), rows)]
    turn = jax.random.randint(jax.random.fold_in(own, 2), (rows, 1), 0, top)
    return jnp.take_along_axis(table, (jnp.arange(top)[None, :] + turn) % top, axis=1)


def shares(number_of, total, reach, slope, full):
    loads = [(1 << 20) // math.isqrt(rank ** slope) + 1 for rank in range(1, number_of + 1)]
    largest = reach if full else min(reach, max(-(-total // number_of), total * loads[0] // sum(loads)))
    least = 1 if total - largest >= number_of - 1 else 0
    holding, spare = [largest] + [least] * (number_of - 1), total - largest - least * (number_of - 1)
    while spare > 0:
        movable = [i for i in range(1, number_of) if holding[i] < largest] or [i for i in range(1, number_of) if holding[i] < reach]
        whole, left = sum([loads[i] for i in movable]), spare
        for i in movable:
            extra = min(reach - holding[i], max(1, left * loads[i] // whole), spare)
            holding[i] = holding[i] + extra
            spare = spare - extra
    return np.array(holding)


def gaussian_with(rng, dims, deviation, limit, split, heavy, kind=jnp.bfloat16):
    drawn = deviation * jax.random.normal(rng, dims, jnp.float32)
    if split:
        drawn = drawn * level_of(rng, dims, split, -0.22, 0.18)
    return jnp.clip(strengthened(drawn, jax.random.fold_in(rng, 3), *heavy), -limit, limit).astype(kind)


def setup_inputs(seed: int = 0, part: int = 0) -> dict:
    streams_of = jax.random.split(jax.random.key(seed), 3)
    part_keys = jax.random.split(jax.random.fold_in(streams_of[2], part), 3)
    tokens = gaussian_with(part_keys[0], (TOKENS, D), 1.0, 6.0, ((0, 16),), (0, 1, 16, 2.0))
    expert_ids_keys = jax.random.split(jax.random.fold_in(part_keys[1], 1), TOKENS // TOK_DEV)
    expert_ids_turns = jax.random.permutation(jax.random.fold_in(part_keys[1], 3), TOKENS // TOK_DEV)
    expert_ids = jax.vmap(lambda own, number: assign_block(jax.random.fold_in(part_keys[1], 2), own, number, TOK_DEV, E_ALL, TOP, CAP, 2))(expert_ids_keys, expert_ids_turns).reshape((TOKENS, TOP))
    return {"tokens": tokens, "expert_ids": expert_ids}


def reference(tokens, expert_ids):
    all_tokens = tokens.shape[0]
    feature_count = tokens.shape[1]
    padded = jnp.concatenate([tokens, jnp.zeros((1, feature_count), tokens.dtype)], axis=0)
    row_limit = N_EXPERT * N_DP * CAP

    def one_expert(expert_index):
        member = jnp.any(expert_ids == expert_index, axis=1)
        member_count = jnp.sum(member.astype(jnp.float32))
        row_index = jnp.nonzero(member, size=row_limit, fill_value=all_tokens)[0]
        chosen = padded[row_index]
        band_cols = chosen[:, :BAND]
        product = lax.dot_general(band_cols, chosen, (((0,), (0,)), ((), ())), preferred_element_type=jnp.float32)
        return product * (2.0 / member_count)

    routed_out = lax.map(one_expert, jnp.arange(WINDOW, dtype=jnp.int32))
    shared_out = lax.dot_general(tokens, tokens[:, :SBAND], (((0,), (0,)), ((), ())), preferred_element_type=jnp.float32)
    shared_out = shared_out * (2.0 / all_tokens)
    return routed_out, shared_out
```

```python
import functools

import jax
import jax.numpy as jnp
from jax import lax
from jax.experimental import pallas as pl
from jax.experimental.pallas import tpu as pltpu
from jax.sharding import PartitionSpec as P

BAND = 384
SBAND = 128
CAP = 8
LANES = 128
VMEM_LIMIT = 32 * 1024 * 1024


def exchange(value, axis, distance):
    size = lax.axis_size(axis)
    return lax.ppermute(value, axis, [(i, i ^ distance) for i in range(size)])


def call(kernel, out_shape, *operands, flops, nbytes, grid_spec=None):
    where = {"grid_spec": grid_spec} if grid_spec is not None else {}
    return pl.pallas_call(
        kernel,
        out_shape=out_shape,
        compiler_params=pltpu.CompilerParams(vmem_limit_bytes=VMEM_LIMIT),
        cost_estimate=pl.CostEstimate(flops=flops, bytes_accessed=nbytes, transcendentals=0),
        **where,
    )(*operands)


def select_kernel(ids_ref, tokens_ref, *out_refs):
    me = lax.axis_index("expert")
    experts = len(out_refs)
    rows, features = tokens_ref.shape
    ids = ids_ref[...]
    members = [
        jnp.max((ids == (me ^ k)).astype(jnp.float32), axis=0, keepdims=True)
        for k in range(experts)
    ]
    member = jnp.concatenate(members, axis=0)
    earlier = (
        lax.broadcasted_iota(jnp.int32, (rows, rows), 0)
        < lax.broadcasted_iota(jnp.int32, (rows, rows), 1)
    ).astype(jnp.bfloat16)
    rank = jnp.dot(member.astype(jnp.bfloat16), earlier, preferred_element_type=jnp.float32)
    slot = lax.broadcasted_iota(jnp.int32, (CAP, rows), 0).astype(jnp.float32)
    picks = jnp.concatenate(
        [
            jnp.where(slot == rank[k : k + 1], member[k : k + 1], 0.0)
            for k in range(experts)
        ],
        axis=0,
    )
    flags = jnp.broadcast_to(jnp.sum(picks, axis=1, keepdims=True), (experts * CAP, LANES))
    chosen = jnp.dot(
        picks.astype(jnp.bfloat16), tokens_ref[...], preferred_element_type=jnp.float32
    )
    for k, out_ref in enumerate(out_refs):
        out_ref[:, :features] = chosen[k * CAP : (k + 1) * CAP].astype(jnp.bfloat16)
        out_ref[:, features:] = flags[k * CAP : (k + 1) * CAP].astype(jnp.bfloat16)


def split_kernel(*refs, peers):
    in_refs, out_refs = refs[:-peers], refs[-peers:]
    me = lax.axis_index("dp")
    features = in_refs[0].shape[1] - LANES
    width = features // peers

    def stacked(columns):
        return jnp.concatenate(
            [ref[:, columns].astype(jnp.float32) for ref in in_refs], axis=0
        ).astype(jnp.bfloat16)

    band = stacked(slice(0, BAND))
    flag = stacked(slice(features, features + LANES))
    for k, out_ref in enumerate(out_refs):
        start = pl.multiple_of((me ^ k) * width, LANES)
        out_ref[:, :width] = stacked(pl.ds(start, width))
        out_ref[:, width : width + BAND] = band
        out_ref[:, width + BAND :] = flag


def hessian_kernel(*refs):
    in_refs, out_ref = refs[:-1], refs[-1]
    width = out_ref.shape[2]
    step = out_ref.shape[1]
    begin = pl.multiple_of(pl.program_id(0) * step, LANES)
    rows = jnp.concatenate([ref[:, :width] for ref in in_refs], axis=0)
    band = jnp.concatenate([ref[:, pl.ds(width + begin, step)] for ref in in_refs], axis=0)
    count = sum(
        jnp.sum(ref[:, width + BAND :].astype(jnp.float32), axis=0, keepdims=True)[:, :1]
        for ref in in_refs
    )
    product = lax.dot_general(
        band, rows, (((0,), (0,)), ((), ())), preferred_element_type=jnp.float32
    )
    out_ref[0] = product * (2.0 / count)


def pair_kernel(mine_ref, other_ref, out_ref):
    features = mine_ref.shape[1]
    block = 4 * LANES
    lead = jnp.concatenate([mine_ref[:, :SBAND], other_ref[:, :SBAND]], axis=0)
    for begin in range(0, features, block):
        part = slice(begin, min(begin + block, features))
        rows = jnp.concatenate([mine_ref[:, part], other_ref[:, part]], axis=0)
        out_ref[part] = lax.dot_general(
            rows, lead, (((0,), (0,)), ((), ())), preferred_element_type=jnp.float32
        )


def on_device(tokens, expert_ids):
    tok_rows, features = tokens.shape
    experts = lax.axis_size("expert")
    peers = lax.axis_size("dp")
    e = lax.axis_index("expert")
    d = lax.axis_index("dp")
    width = features // peers
    share = features // (experts * peers)

    other = exchange(tokens, "dp", 1)

    outgoing = call(
        select_kernel,
        [jax.ShapeDtypeStruct((CAP, features + LANES), jnp.bfloat16)] * experts,
        expert_ids.T,
        tokens,
        flops=2 * experts * CAP * tok_rows * features,
        nbytes=2 * (tok_rows + experts * CAP) * features,
    )
    arrived = [outgoing[0]] + [exchange(outgoing[k], "expert", k) for k in range(1, experts)]

    pair = call(
        pair_kernel,
        jax.ShapeDtypeStruct((features, SBAND), jnp.float32),
        tokens,
        other,
        flops=4 * tok_rows * features * SBAND,
        nbytes=4 * tok_rows * features + 4 * features * SBAND,
    )

    def block(m, k):
        start = ((e ^ m) * peers + (d ^ k)) * share
        return lax.dynamic_slice_in_dim(pair, start, share, axis=0)

    def over_dp(m):
        far = [exchange(block(m, k), "dp", k) for k in range(2, peers, 2)]
        return sum(far, block(m, 0))

    order = list(range(3, experts, 2)) + list(range(2, experts, 2)) + [1, 0]
    part = {m: over_dp(m) for m in order}
    for m in range(2, experts, 2):
        part[m] = part[m] + exchange(part[m + 1], "expert", 1)
    summed = part[0] + exchange(part[1], "expert", 1)
    for m in range(2, experts, 2):
        summed = summed + exchange(part[m], "expert", m)
    shared_out = summed * (2.0 / (tok_rows * experts * peers))

    wide = width + BAND + LANES
    packed = call(
        functools.partial(split_kernel, peers=peers),
        [jax.ShapeDtypeStruct((experts * CAP, wide), jnp.bfloat16)] * peers,
        *arrived,
        flops=0,
        nbytes=4 * experts * CAP * features,
    )
    gathered = [packed[0]] + [exchange(packed[k], "dp", k) for k in range(1, peers)]
    steps = BAND // LANES
    routed_out = call(
        hessian_kernel,
        jax.ShapeDtypeStruct((1, BAND, width), jnp.float32),
        *gathered,
        flops=2 * BAND * width * experts * peers * CAP,
        nbytes=4 * BAND * width,
        grid_spec=pl.GridSpec(
            grid=(steps,),
            in_specs=[pl.BlockSpec((experts * CAP, wide), lambda i: (0, 0))] * peers,
            out_specs=pl.BlockSpec((1, BAND // steps, width), lambda i: (0, i, 0)),
        ),
    )
    return routed_out, shared_out


def solution(mesh):
    in_specs = (P(("groups", "expert", "dp"), None), P(("groups", "expert", "dp"), None))
    out_specs = (P(("groups", "expert"), None, "dp"), P(("groups", "expert", "dp"), None))
    return jax.shard_map(
        on_device, mesh=mesh, in_specs=in_specs, out_specs=out_specs, check_vma=False
    )
```

```python
import functools

import jax
import jax.numpy as jnp
from jax import lax
from jax.experimental import pallas as pl
from jax.experimental.pallas import tpu as pltpu
from jax.sharding import PartitionSpec as P

BAND = 384
SBAND = 128
CAP = 8
LANES = 128
VMEM_LIMIT = 16 * 1024 * 1024


def exchange(value, axis, distance):
    size = lax.axis_size(axis)
    return lax.ppermute(value, axis, [(i, i ^ distance) for i in range(size)])


def call(kernel, out_shape, *operands, flops, nbytes, **where):
    return pl.pallas_call(
        kernel,
        out_shape=out_shape,
        compiler_params=pltpu.CompilerParams(vmem_limit_bytes=VMEM_LIMIT),
        cost_estimate=pl.CostEstimate(flops=flops, bytes_accessed=nbytes, transcendentals=0),
        **where,
    )(*operands)


def parts_of(features):
    step = -(-features // (4 * LANES)) * LANES
    return [slice(b, min(b + step, features)) for b in range(0, features, step)]


def select_kernel(ids_ref, tokens_ref, *refs):
    out_refs, held, sems = refs[:-2], refs[-2], refs[-1]
    me = lax.axis_index("expert")
    experts = len(out_refs)
    rows, features = tokens_ref.shape
    parts = parts_of(features)
    copies = [
        pltpu.make_async_copy(tokens_ref.at[:, part], held.at[:, part], sems.at[i])
        for i, part in enumerate(parts)
    ]
    for copy in copies:
        copy.start()
    ids = ids_ref[...]
    members = [
        jnp.max((ids == (me ^ k)).astype(jnp.float32), axis=0, keepdims=True)
        for k in range(experts)
    ]
    member = jnp.concatenate(members, axis=0)
    earlier = (
        lax.broadcasted_iota(jnp.int32, (rows, rows), 0)
        < lax.broadcasted_iota(jnp.int32, (rows, rows), 1)
    ).astype(jnp.bfloat16)
    rank = jnp.dot(member.astype(jnp.bfloat16), earlier, preferred_element_type=jnp.float32)
    slot = lax.broadcasted_iota(jnp.int32, (CAP, rows), 0).astype(jnp.float32)
    picks = jnp.concatenate(
        [
            jnp.where(slot == rank[k : k + 1], member[k : k + 1], 0.0)
            for k in range(experts)
        ],
        axis=0,
    )
    flags = jnp.broadcast_to(jnp.sum(picks, axis=1, keepdims=True), (experts * CAP, LANES))
    picks = picks.astype(jnp.bfloat16)
    for k, out_ref in enumerate(out_refs):
        out_ref[:, features:] = flags[k * CAP : (k + 1) * CAP].astype(jnp.bfloat16)
    for copy, part in zip(copies, parts):
        copy.wait()
        chosen = jnp.dot(picks, held[:, part], preferred_element_type=jnp.float32)
        for k, out_ref in enumerate(out_refs):
            out_ref[:, part] = chosen[k * CAP : (k + 1) * CAP].astype(jnp.bfloat16)


def split_kernel(*refs, peers):
    in_refs, out_refs = refs[:-peers], refs[-peers:]
    me = lax.axis_index("dp")
    features = in_refs[0].shape[1] - LANES
    width = features // peers

    def stacked(columns):
        return jnp.concatenate(
            [ref[:, columns].astype(jnp.float32) for ref in in_refs], axis=0
        ).astype(jnp.bfloat16)

    band = stacked(slice(0, BAND))
    flag = stacked(slice(features, features + LANES))
    for k, out_ref in enumerate(out_refs):
        start = pl.multiple_of((me ^ k) * width, LANES)
        out_ref[:, :width] = stacked(pl.ds(start, width))
        out_ref[:, width : width + BAND] = band
        out_ref[:, width + BAND :] = flag


def hessian_kernel(*refs):
    in_refs, out_ref = refs[:-1], refs[-1]
    width = out_ref.shape[2]
    step = out_ref.shape[1]
    begin = pl.multiple_of(pl.program_id(0) * step, LANES)
    rows = jnp.concatenate([ref[:, :width] for ref in in_refs], axis=0)
    band = jnp.concatenate([ref[:, pl.ds(width + begin, step)] for ref in in_refs], axis=0)
    count = sum(
        jnp.sum(ref[:, width + BAND :].astype(jnp.float32), axis=0, keepdims=True)[:, :1]
        for ref in in_refs
    )
    product = lax.dot_general(
        band, rows, (((0,), (0,)), ((), ())), preferred_element_type=jnp.float32
    )
    out_ref[0] = product * (2.0 / count)


def pair_kernel(mine_ref, other_ref, *refs, experts, peers, order, aligned):
    out_refs, mine, other, sems = refs[:-3], refs[-3], refs[-2], refs[-1]
    features = mine_ref.shape[1]
    parts = parts_of(features)
    copies = [
        (
            pltpu.make_async_copy(mine_ref.at[:, part], mine.at[:, part], sems.at[0, i]),
            pltpu.make_async_copy(other_ref.at[:, part], other.at[:, part], sems.at[1, i]),
        )
        for i, part in enumerate(parts)
    ]
    for pair in copies:
        for copy in pair:
            copy.start()
    for pair in copies:
        for copy in pair:
            copy.wait()
    lead = jnp.concatenate([mine[:, :SBAND], other[:, :SBAND]], axis=0)

    def product(columns):
        rows = jnp.concatenate([mine[:, columns], other[:, columns]], axis=0)
        return lax.dot_general(
            rows, lead, (((0,), (0,)), ((), ())), preferred_element_type=jnp.float32
        )

    if not aligned:
        for part in parts:
            out_refs[0][part] = product(part)
        return
    e = lax.axis_index("expert")
    d = lax.axis_index("dp")
    share = features // (experts * peers)
    half = LANES // 2
    window = share + half * (share // half % 2)
    for i, m in enumerate(order):
        for j, k in enumerate(range(0, peers, 2)):
            start = ((e ^ m) * peers + (d ^ k)) * (share // half)
            odd = start % 2
            found = product(pl.ds(pl.multiple_of((start - odd) * half, LANES), window))
            if window > share:
                found = jnp.where(odd == 1, found[half:], found[:share])
            out_refs[i * (peers // 2) + j][...] = found


def on_device(tokens, expert_ids):
    tok_rows, features = tokens.shape
    experts = lax.axis_size("expert")
    peers = lax.axis_size("dp")
    width = features // peers
    share = features // (experts * peers)
    steps = len(parts_of(features))
    whole = pl.BlockSpec(memory_space=pltpu.HBM)
    inside = pl.BlockSpec(memory_space=pltpu.VMEM)

    other = exchange(tokens, "dp", 1)

    outgoing = call(
        select_kernel,
        [jax.ShapeDtypeStruct((CAP, features + LANES), jnp.bfloat16)] * experts,
        expert_ids.T,
        tokens,
        flops=2 * experts * CAP * tok_rows * features,
        nbytes=2 * (tok_rows + experts * CAP) * features,
        in_specs=[inside, whole],
        scratch_shapes=[
            pltpu.VMEM((tok_rows, features), jnp.bfloat16),
            pltpu.SemaphoreType.DMA((steps,)),
        ],
    )
    outgoing, other = lax.optimization_barrier((outgoing, other))

    order = list(range(3, experts, 2)) + list(range(2, experts, 2)) + [1, 0]
    aligned = share % (LANES // 2) == 0
    blocks = call(
        functools.partial(
            pair_kernel, experts=experts, peers=peers, order=order, aligned=aligned
        ),
        [jax.ShapeDtypeStruct((share, SBAND), jnp.float32)] * (experts * peers // 2)
        if aligned
        else [jax.ShapeDtypeStruct((features, SBAND), jnp.float32)],
        tokens,
        other,
        flops=4 * tok_rows * features * SBAND,
        nbytes=4 * tok_rows * features + 4 * features * SBAND,
        in_specs=[whole, whole],
        scratch_shapes=[
            pltpu.VMEM((tok_rows, features), jnp.bfloat16),
            pltpu.VMEM((tok_rows, features), jnp.bfloat16),
            pltpu.SemaphoreType.DMA((2, steps)),
        ],
    )
    if not aligned:
        e, d = lax.axis_index("expert"), lax.axis_index("dp")
        blocks = [
            lax.dynamic_slice_in_dim(
                blocks[0], ((e ^ m) * peers + (d ^ k)) * share, share, axis=0
            )
            for m in order
            for k in range(0, peers, 2)
        ]
    outgoing, blocks = lax.optimization_barrier((outgoing, blocks))

    part = {}
    for i, m in enumerate(order):
        own, *sent = blocks[i * (peers // 2) : (i + 1) * (peers // 2)]
        part[m] = sum([exchange(x, "dp", 2 * k + 2) for k, x in enumerate(sent)], own)
    arrived = [outgoing[0]] + [exchange(outgoing[k], "expert", k) for k in range(1, experts)]
    for m in range(2, experts, 2):
        part[m] = part[m] + exchange(part[m + 1], "expert", 1)
    summed = part[0] + exchange(part[1], "expert", 1)
    for m in range(2, experts, 2):
        summed = summed + exchange(part[m], "expert", m)
    shared_out = summed * (2.0 / (tok_rows * experts * peers))

    wide = width + BAND + LANES
    packed = call(
        functools.partial(split_kernel, peers=peers),
        [jax.ShapeDtypeStruct((experts * CAP, wide), jnp.bfloat16)] * peers,
        *arrived,
        flops=0,
        nbytes=4 * experts * CAP * features,
    )
    gathered = [packed[0]] + [exchange(packed[k], "dp", k) for k in range(1, peers)]
    steps = BAND // LANES
    routed_out = call(
        hessian_kernel,
        jax.ShapeDtypeStruct((1, BAND, width), jnp.float32),
        *gathered,
        flops=2 * BAND * width * experts * peers * CAP,
        nbytes=4 * BAND * width,
        grid_spec=pl.GridSpec(
            grid=(steps,),
            in_specs=[pl.BlockSpec((experts * CAP, wide), lambda i: (0, 0))] * peers,
            out_specs=pl.BlockSpec((1, BAND // steps, width), lambda i: (0, i, 0)),
        ),
    )
    return routed_out, shared_out


def solution(mesh):
    in_specs = (P(("groups", "expert", "dp"), None), P(("groups", "expert", "dp"), None))
    out_specs = (P(("groups", "expert"), None, "dp"), P(("groups", "expert", "dp"), None))
    return jax.shard_map(
        on_device, mesh=mesh, in_specs=in_specs, out_specs=out_specs, check_vma=False
    )
```

```python
import functools

import jax
import jax.numpy as jnp
from jax import lax
from jax.experimental import pallas as pl
from jax.experimental.pallas import tpu as pltpu
from jax.sharding import PartitionSpec as P

BAND = 384
SBAND = 128
CAP = 8
LANES = 128
PAD = 16
VMEM_LIMIT = 16 * 1024 * 1024


def exchange(value, axis, distance):
    size = lax.axis_size(axis)
    return lax.ppermute(value, axis, [(i, i ^ distance) for i in range(size)])


def tie(value, after):
    return value if after is None else lax.optimization_barrier((value, after))[0]


def pass_on(value, distance):
    experts, peers = lax.axis_size("expert"), lax.axis_size("dp")
    pairs = [
        (e * peers + d, (e ^ (distance + d % 2)) * peers + d)
        for e in range(experts)
        for d in range(peers)
        if distance + d % 2
    ]
    return lax.ppermute(value, ("expert", "dp"), pairs)


def call(kernel, out_shape, *operands, flops, nbytes, **where):
    return pl.pallas_call(
        kernel,
        out_shape=out_shape,
        compiler_params=pltpu.CompilerParams(vmem_limit_bytes=VMEM_LIMIT),
        cost_estimate=pl.CostEstimate(flops=flops, bytes_accessed=nbytes, transcendentals=0),
        **where,
    )(*operands)


def parts_of(features):
    step = -(-features // (4 * LANES)) * LANES
    return [slice(b, min(b + step, features)) for b in range(0, features, step)]


def split_kernel(*refs, peers):
    in_refs, out_refs = refs[: -1 - peers // 2], refs[-1 - peers // 2 :]
    me = lax.axis_index("dp")
    features = in_refs[0].shape[1] - LANES
    width = features // peers

    def stacked(columns):
        return jnp.concatenate([ref[:, columns] for ref in in_refs], axis=0)

    def columns_of(k):
        return stacked(pl.ds(pl.multiple_of((me ^ k) * width, LANES), width))

    band = stacked(slice(0, BAND))
    flag = stacked(slice(features, features + LANES))
    for ref, pieces in zip(out_refs, [[0], [1]] + [[k, k + 1] for k in range(2, peers, 2)]):
        for i, k in enumerate(pieces):
            ref[:, i * width : (i + 1) * width] = columns_of(k)
        end = len(pieces) * width
        ref[:, end : end + BAND] = band
        ref[:, end + BAND :] = flag


def hessian_kernel(*refs, width):
    in_refs, out_ref = refs[:-1], refs[-1]
    step = out_ref.shape[1]
    begin = pl.program_id(0) * step

    def tail(ref, start, size):
        start = pl.multiple_of(ref.shape[1] - BAND - LANES + start, LANES)
        return ref[:, pl.ds(start, size)]

    rows = jnp.concatenate([ref[:, :width] for ref in in_refs], axis=0)
    band = jnp.concatenate([tail(ref, begin, step) for ref in in_refs], axis=0)
    count = sum(
        jnp.sum(tail(ref, BAND, LANES).astype(jnp.float32), axis=0, keepdims=True)[:, :1]
        for ref in in_refs
    )
    product = lax.dot_general(
        band, rows, (((0,), (0,)), ((), ())), preferred_element_type=jnp.float32
    )
    out_ref[0] = product * (2.0 / count)


def select(ids, expert):
    tokens = ids.shape[1]
    member = jnp.max((ids == expert).astype(jnp.float32), axis=0, keepdims=True)
    earlier = (
        lax.broadcasted_iota(jnp.int32, (tokens, tokens), 0)
        < lax.broadcasted_iota(jnp.int32, (tokens, tokens), 1)
    ).astype(jnp.bfloat16)
    rank = jnp.dot(member.astype(jnp.bfloat16), earlier, preferred_element_type=jnp.float32)
    slot = lax.broadcasted_iota(jnp.int32, (2 * CAP, tokens), 0).astype(jnp.float32)
    return jnp.where(slot == rank, member, 0.0)


def fetch_kernel(ids_ref, tokens_ref, held_ids_ref, held_ref, sems):
    copies = [
        pltpu.make_async_copy(ids_ref, held_ids_ref, sems.at[0]),
        pltpu.make_async_copy(tokens_ref, held_ref, sems.at[1]),
    ]
    for copy in copies:
        copy.start()
    for copy in copies:
        copy.wait()


def pair_kernel(
    ids_ref, other_ids_ref, mine_ref, other_ref, *out_refs, experts, peers, wanted, aligned
):
    out_refs, row_refs = out_refs[: -experts // 2], out_refs[-experts // 2 :]
    features = mine_ref.shape[1]
    e = lax.axis_index("expert")
    d = lax.axis_index("dp")

    def both(columns):
        return jnp.concatenate([mine_ref[:, columns], other_ref[:, columns]], axis=0)

    lead = both(slice(0, SBAND))

    def product(columns):
        return lax.dot_general(
            both(columns), lead, (((0,), (0,)), ((), ())), preferred_element_type=jnp.float32
        )

    if aligned:
        share = features // (experts * peers)
        half = LANES // 2
        window = share + half * (share // half % 2)
        for out_ref, pairs in zip(out_refs, wanted):
            for i, (m, k) in enumerate(pairs):
                start = ((e ^ m) * peers + (d ^ k)) * (share // half)
                odd = start % 2
                found = product(pl.ds(pl.multiple_of((start - odd) * half, LANES), window))
                if window > share:
                    found = jnp.where(odd == 1, found[half:], found[:share])
                out_ref[i * share : (i + 1) * share] = found
            filled = len(pairs) * share
            if out_ref.shape[0] > filled:
                out_ref[filled:] = jnp.zeros_like(out_ref[filled:])
    else:
        for part in parts_of(features):
            out_refs[0][part] = product(part)

    ids = jnp.concatenate([ids_ref[...], other_ids_ref[...]], axis=1)
    picks = jnp.concatenate(
        [select(ids, e ^ (k + d % 2)) for k in range(0, experts, 2)], axis=0
    )
    flags = jnp.broadcast_to(jnp.sum(picks, axis=1, keepdims=True), (picks.shape[0], LANES))
    picks = picks.astype(jnp.bfloat16)
    for part in parts_of(features):
        chosen = jnp.dot(picks, both(part), preferred_element_type=jnp.float32)
        for i, ref in enumerate(row_refs):
            ref[:, part] = chosen[2 * CAP * i : 2 * CAP * (i + 1)].astype(jnp.bfloat16)
    for i, ref in enumerate(row_refs):
        ref[:, features:] = flags[2 * CAP * i : 2 * CAP * (i + 1)].astype(jnp.bfloat16)


def on_device(tokens, expert_ids):
    tok_rows, features = tokens.shape
    experts = lax.axis_size("expert")
    peers = lax.axis_size("dp")
    width = features // peers
    share = features // (experts * peers)
    anywhere = pl.BlockSpec(memory_space=pl.ANY)
    inside = pl.BlockSpec(memory_space=pltpu.VMEM)

    ids = expert_ids.T
    other = exchange(tokens, "dp", 1)
    other_ids = exchange(ids, "dp", 1)
    ids, mine = call(
        fetch_kernel,
        [
            jax.ShapeDtypeStruct(ids.shape, ids.dtype),
            jax.ShapeDtypeStruct(tokens.shape, tokens.dtype),
        ],
        ids,
        tokens,
        flops=0,
        nbytes=4 * tok_rows * features,
        in_specs=[anywhere, anywhere],
        out_specs=[inside, inside],
        scratch_shapes=[pltpu.SemaphoreType.DMA((2,))],
    )
    ids, mine, other, other_ids = lax.optimization_barrier((ids, mine, other, other_ids))

    even = range(0, peers, 2)
    far = range(2, experts, 2)
    groups = [[m + 1 for m in far], [*far], [1], [0]]
    wanted = [[(m, k) for m in group] for group in groups for k in even]
    aligned = share % (LANES // 2) == 0
    sizes = [len(pairs) * share for pairs in wanted]
    for i in range(1, peers // 2):
        sizes[i] += PAD
    found = call(
        functools.partial(
            pair_kernel, experts=experts, peers=peers, wanted=wanted, aligned=aligned
        ),
        [
            jax.ShapeDtypeStruct((size, SBAND), jnp.float32)
            for size in (sizes if aligned else [features])
        ]
        + [jax.ShapeDtypeStruct((2 * CAP, features + LANES), jnp.bfloat16)] * (experts // 2),
        ids,
        other_ids,
        mine,
        other,
        flops=4 * tok_rows * features * (SBAND + experts * CAP),
        nbytes=4 * tok_rows * features + 4 * features * SBAND,
    )
    blocks, outgoing = found[: -experts // 2], found[-experts // 2 :]
    if not aligned:
        e, d = lax.axis_index("expert"), lax.axis_index("dp")
        blocks = [
            jnp.concatenate(
                [
                    lax.dynamic_slice_in_dim(
                        blocks[0], ((e ^ m) * peers + (d ^ k)) * share, share, axis=0
                    )
                    for m, k in pairs
                ],
                axis=0,
            )
            for pairs in wanted
        ]
    def over_dp(i, after=None):
        own, *sent = blocks[i * (peers // 2) : (i + 1) * (peers // 2)]
        got = [exchange(tie(x, after), "dp", 2 * k + 2) for k, x in enumerate(sent)]
        return sum([x[: own.shape[0]] for x in got], own)

    near = exchange(over_dp(0), "expert", 1)
    paired = over_dp(1) + near
    beside_sum = exchange(over_dp(2), "expert", 1)
    own = over_dp(3, near) + beside_sum

    arrived = [pass_on(outgoing[k], 2 * k) for k in range(experts // 2)]
    arrived[0] = jnp.where(lax.axis_index("dp") % 2 == 0, outgoing[0], arrived[0])

    rows = experts * CAP
    tail = BAND + LANES
    mine, give, *packed = call(
        functools.partial(split_kernel, peers=peers),
        [jax.ShapeDtypeStruct((rows, width + tail), jnp.bfloat16)] * 2
        + [jax.ShapeDtypeStruct((rows, 2 * width + tail), jnp.bfloat16)] * (peers // 2 - 1),
        *arrived,
        flops=0,
        nbytes=4 * rows * features,
    )
    across = [exchange(x, "dp", 2 * k + 2) for k, x in enumerate(packed)]
    beside = exchange(jnp.concatenate([give] + [x[:, width:] for x in across]), "dp", 1)
    gathered = [mine, *across, beside]
    steps = BAND // LANES
    routed_out = call(
        functools.partial(hessian_kernel, width=width),
        jax.ShapeDtypeStruct((1, BAND, width), jnp.float32),
        *gathered,
        flops=2 * BAND * width * rows * peers,
        nbytes=4 * BAND * width,
        grid_spec=pl.GridSpec(
            grid=(steps,),
            in_specs=[pl.BlockSpec(x.shape, lambda i: (0, 0)) for x in gathered],
            out_specs=pl.BlockSpec((1, BAND // steps, width), lambda i: (0, i, 0)),
        ),
    )
    paired = tie(paired, packed)
    others = [
        exchange(paired[i * share : (i + 1) * share], "expert", m) for i, m in enumerate(far)
    ]
    summed = sum(others, lax.optimization_barrier(own))
    shared_out = summed * (2.0 / (tok_rows * experts * peers))
    return routed_out, shared_out


def solution(mesh):
    in_specs = (P(("groups", "expert", "dp"), None), P(("groups", "expert", "dp"), None))
    out_specs = (P(("groups", "expert"), None, "dp"), P(("groups", "expert", "dp"), None))
    return jax.shard_map(
        on_device, mesh=mesh, in_specs=in_specs, out_specs=out_specs, check_vma=False
    )
```

```python
import functools

import jax
import jax.numpy as jnp
from jax import lax
from jax.experimental import pallas as pl
from jax.experimental.pallas import tpu as pltpu
from jax.sharding import PartitionSpec as P

BAND = 384
SBAND = 128
CAP = 8
LANES = 128
PAD = 16
VMEM_LIMIT = 16 * 1024 * 1024


def exchange(value, axis, distance):
    size = lax.axis_size(axis)
    return lax.ppermute(value, axis, [(i, i ^ distance) for i in range(size)])


def tie(value, after):
    return value if after is None else lax.optimization_barrier((value, after))[0]


def pass_on(value, distance):
    experts, peers = lax.axis_size("expert"), lax.axis_size("dp")
    pairs = [
        (e * peers + d, (e ^ (distance + d % 2)) * peers + d)
        for e in range(experts)
        for d in range(peers)
        if distance + d % 2
    ]
    return lax.ppermute(value, ("expert", "dp"), pairs)


def call(kernel, out_shape, *operands, flops, nbytes, **where):
    return pl.pallas_call(
        kernel,
        out_shape=out_shape,
        compiler_params=pltpu.CompilerParams(vmem_limit_bytes=VMEM_LIMIT),
        cost_estimate=pl.CostEstimate(flops=flops, bytes_accessed=nbytes, transcendentals=0),
        **where,
    )(*operands)


def parts_of(features):
    step = -(-features // (4 * LANES)) * LANES
    return [slice(b, min(b + step, features)) for b in range(0, features, step)]


def split_kernel(*refs, peers):
    in_refs, out_refs = refs[: -1 - peers // 2], refs[-1 - peers // 2 :]
    me = lax.axis_index("dp")
    features = in_refs[0].shape[1] - LANES
    width = features // peers

    def stacked(columns):
        return jnp.concatenate([ref[:, columns] for ref in in_refs], axis=0)

    def columns_of(k):
        return stacked(pl.ds(pl.multiple_of((me ^ k) * width, LANES), width))

    band = stacked(slice(0, BAND))
    flag = stacked(slice(features, features + LANES))
    for ref, pieces in zip(out_refs, [[0], [1]] + [[k, k + 1] for k in range(2, peers, 2)]):
        for i, k in enumerate(pieces):
            ref[:, i * width : (i + 1) * width] = columns_of(k)
        end = len(pieces) * width
        ref[:, end : end + BAND] = band
        ref[:, end + BAND :] = flag


def hessian_kernel(*refs):
    row_refs, (routed_ref, routed, sems) = refs[:-3], refs[-3:]
    _, band_size, width = routed_ref.shape
    copies = []

    def send(source, target):
        copies.append(pltpu.make_async_copy(source, target, sems.at[len(copies)]))
        copies[-1].start()

    def tail(ref, start, size):
        start += ref.shape[1] - BAND - LANES
        return ref[:, start : start + size]

    rows = jnp.concatenate([ref[:, :width] for ref in row_refs], axis=0)
    band = jnp.concatenate([tail(ref, 0, BAND) for ref in row_refs], axis=0)
    count = sum(
        jnp.sum(tail(ref, BAND, LANES).astype(jnp.float32), axis=0, keepdims=True)[:, :1]
        for ref in row_refs
    )
    for begin in range(0, band_size, LANES):
        part = slice(begin, begin + LANES)
        product = lax.dot_general(
            band[:, part], rows, (((0,), (0,)), ((), ())), preferred_element_type=jnp.float32
        )
        routed[part] = product * (2.0 / count)
        send(routed.at[part], routed_ref.at[0, part])
    for copy in copies:
        copy.wait()


def select(ids, expert):
    tokens = ids.shape[1]
    member = jnp.max((ids == expert).astype(jnp.float32), axis=0, keepdims=True)
    earlier = (
        lax.broadcasted_iota(jnp.int32, (tokens, tokens), 0)
        < lax.broadcasted_iota(jnp.int32, (tokens, tokens), 1)
    ).astype(jnp.bfloat16)
    rank = jnp.dot(member.astype(jnp.bfloat16), earlier, preferred_element_type=jnp.float32)
    slot = lax.broadcasted_iota(jnp.int32, (2 * CAP, tokens), 0).astype(jnp.float32)
    return jnp.where(slot == rank, member, 0.0)


def fetch_kernel(ids_ref, tokens_ref, held_ids_ref, held_ref, sems):
    copies = [
        pltpu.make_async_copy(ids_ref, held_ids_ref, sems.at[0]),
        pltpu.make_async_copy(tokens_ref, held_ref, sems.at[1]),
    ]
    for copy in copies:
        copy.start()
    for copy in copies:
        copy.wait()


def pair_kernel(
    ids_ref, other_ids_ref, mine_ref, other_ref, *out_refs, experts, peers, wanted, aligned
):
    out_refs, row_refs = out_refs[: -experts // 2], out_refs[-experts // 2 :]
    features = mine_ref.shape[1]
    e = lax.axis_index("expert")
    d = lax.axis_index("dp")

    def both(columns):
        return jnp.concatenate([mine_ref[:, columns], other_ref[:, columns]], axis=0)

    lead = both(slice(0, SBAND))

    def product(columns):
        return lax.dot_general(
            both(columns), lead, (((0,), (0,)), ((), ())), preferred_element_type=jnp.float32
        )

    if aligned:
        share = features // (experts * peers)
        half = LANES // 2
        window = share + half * (share // half % 2)
        for out_ref, pairs in zip(out_refs, wanted):
            for i, (m, k) in enumerate(pairs):
                start = ((e ^ m) * peers + (d ^ k)) * (share // half)
                odd = start % 2
                found = product(pl.ds(pl.multiple_of((start - odd) * half, LANES), window))
                if window > share:
                    found = jnp.where(odd == 1, found[half:], found[:share])
                out_ref[i * share : (i + 1) * share] = found
            filled = len(pairs) * share
            if out_ref.shape[0] > filled:
                out_ref[filled:] = jnp.zeros_like(out_ref[filled:])
    else:
        for part in parts_of(features):
            out_refs[0][part] = product(part)

    ids = jnp.concatenate([ids_ref[...], other_ids_ref[...]], axis=1)
    picks = jnp.concatenate(
        [select(ids, e ^ (k + d % 2)) for k in range(0, experts, 2)], axis=0
    )
    flags = jnp.broadcast_to(jnp.sum(picks, axis=1, keepdims=True), (picks.shape[0], LANES))
    picks = picks.astype(jnp.bfloat16)
    for part in parts_of(features):
        chosen = jnp.dot(picks, both(part), preferred_element_type=jnp.float32)
        for i, ref in enumerate(row_refs):
            ref[:, part] = chosen[2 * CAP * i : 2 * CAP * (i + 1)].astype(jnp.bfloat16)
    for i, ref in enumerate(row_refs):
        ref[:, features:] = flags[2 * CAP * i : 2 * CAP * (i + 1)].astype(jnp.bfloat16)


def on_device(tokens, expert_ids):
    tok_rows, features = tokens.shape
    experts = lax.axis_size("expert")
    peers = lax.axis_size("dp")
    width = features // peers
    share = features // (experts * peers)
    anywhere = pl.BlockSpec(memory_space=pl.ANY)
    inside = pl.BlockSpec(memory_space=pltpu.VMEM)

    ids = expert_ids.T
    other = exchange(tokens, "dp", 1)
    other_ids = exchange(ids, "dp", 1)
    ids, mine = call(
        fetch_kernel,
        [
            jax.ShapeDtypeStruct(ids.shape, ids.dtype),
            jax.ShapeDtypeStruct(tokens.shape, tokens.dtype),
        ],
        ids,
        tokens,
        flops=0,
        nbytes=4 * tok_rows * features,
        in_specs=[anywhere, anywhere],
        out_specs=[inside, inside],
        scratch_shapes=[pltpu.SemaphoreType.DMA((2,))],
    )
    ids, mine, other, other_ids = lax.optimization_barrier((ids, mine, other, other_ids))

    even = range(0, peers, 2)
    far = range(2, experts, 2)
    groups = [[m + 1 for m in far], [*far], [1], [0]]
    wanted = [[(m, k) for m in group] for group in groups for k in even]
    aligned = share % (LANES // 2) == 0
    sizes = [len(pairs) * share for pairs in wanted]
    for i in range(1, peers // 2):
        sizes[i] += PAD
    found = call(
        functools.partial(
            pair_kernel, experts=experts, peers=peers, wanted=wanted, aligned=aligned
        ),
        [
            jax.ShapeDtypeStruct((size, SBAND), jnp.float32)
            for size in (sizes if aligned else [features])
        ]
        + [jax.ShapeDtypeStruct((2 * CAP, features + LANES), jnp.bfloat16)] * (experts // 2),
        ids,
        other_ids,
        mine,
        other,
        flops=4 * tok_rows * features * (SBAND + experts * CAP),
        nbytes=4 * tok_rows * features + 4 * features * SBAND,
    )
    blocks, outgoing = found[: -experts // 2], found[-experts // 2 :]
    if not aligned:
        e, d = lax.axis_index("expert"), lax.axis_index("dp")
        blocks = [
            jnp.concatenate(
                [
                    lax.dynamic_slice_in_dim(
                        blocks[0], ((e ^ m) * peers + (d ^ k)) * share, share, axis=0
                    )
                    for m, k in pairs
                ],
                axis=0,
            )
            for pairs in wanted
        ]
    def over_dp(i, after=None):
        own, *sent = blocks[i * (peers // 2) : (i + 1) * (peers // 2)]
        got = [exchange(tie(x, after), "dp", 2 * k + 2) for k, x in enumerate(sent)]
        return sum([x[: own.shape[0]] for x in got], own)

    odd = over_dp(0)
    near = exchange(odd, "expert", 1)
    paired = over_dp(1, odd) + near
    beside_sum = exchange(over_dp(2), "expert", 1)
    own = over_dp(3, near) + beside_sum

    arrived = [pass_on(outgoing[k], 2 * k) for k in range(experts // 2)]
    arrived[0] = jnp.where(lax.axis_index("dp") % 2 == 0, outgoing[0], arrived[0])

    rows = experts * CAP
    tail = BAND + LANES
    mine, give, *packed = call(
        functools.partial(split_kernel, peers=peers),
        [jax.ShapeDtypeStruct((rows, width + tail), jnp.bfloat16)] * 2
        + [jax.ShapeDtypeStruct((rows, 2 * width + tail), jnp.bfloat16)] * (peers // 2 - 1),
        *arrived,
        flops=0,
        nbytes=4 * rows * features,
    )
    across = [exchange(x, "dp", 2 * k + 2) for k, x in enumerate(packed)]
    beside = exchange(jnp.concatenate([give] + [x[:, width:] for x in across]), "dp", 1)
    gathered = [mine, *across, beside]
    routed_out = call(
        hessian_kernel,
        jax.ShapeDtypeStruct((1, BAND, width), jnp.float32),
        *gathered,
        flops=2 * BAND * width * rows * peers,
        nbytes=4 * BAND * width,
        in_specs=[inside] * len(gathered),
        out_specs=anywhere,
        scratch_shapes=[
            pltpu.VMEM((BAND, width), jnp.float32),
            pltpu.SemaphoreType.DMA((BAND // LANES,)),
        ],
    )
    paired = tie(paired, packed)
    others = [
        exchange(paired[i * share : (i + 1) * share], "expert", m) for i, m in enumerate(far)
    ]
    summed = sum(others, lax.optimization_barrier(own))
    shared_out = summed * (2.0 / (tok_rows * experts * peers))
    return routed_out, shared_out


def solution(mesh):
    in_specs = (P(("groups", "expert", "dp"), None), P(("groups", "expert", "dp"), None))
    out_specs = (P(("groups", "expert"), None, "dp"), P(("groups", "expert", "dp"), None))
    return jax.shard_map(
        on_device, mesh=mesh, in_specs=in_specs, out_specs=out_specs, check_vma=False
    )
```

```python
import functools

import jax
import jax.numpy as jnp
from jax import lax
from jax.experimental import pallas as pl
from jax.experimental.pallas import tpu as pltpu
from jax.sharding import PartitionSpec as P

BAND = 384
SBAND = 128
CAP = 8
LANES = 128
PAD = 16
VMEM_LIMIT = 16 * 1024 * 1024


def exchange(value, axis, distance):
    size = lax.axis_size(axis)
    return lax.ppermute(value, axis, [(i, i ^ distance) for i in range(size)])


def tie(value, after):
    return value if after is None else lax.optimization_barrier((value, after))[0]


def pass_on(value, distance):
    experts, peers = lax.axis_size("expert"), lax.axis_size("dp")
    pairs = [
        (e * peers + d, (e ^ (distance + d % 2)) * peers + d)
        for e in range(experts)
        for d in range(peers)
        if distance + d % 2
    ]
    return lax.ppermute(value, ("expert", "dp"), pairs)


def call(kernel, out_shape, *operands, flops, nbytes, **where):
    return pl.pallas_call(
        kernel,
        out_shape=out_shape,
        compiler_params=pltpu.CompilerParams(vmem_limit_bytes=VMEM_LIMIT),
        cost_estimate=pl.CostEstimate(flops=flops, bytes_accessed=nbytes, transcendentals=0),
        **where,
    )(*operands)


def parts_of(features):
    step = -(-features // (4 * LANES)) * LANES
    return [slice(b, min(b + step, features)) for b in range(0, features, step)]


def split_kernel(*refs, peers):
    in_refs, out_refs = refs[: -1 - peers // 2], refs[-1 - peers // 2 :]
    me = lax.axis_index("dp")
    features = in_refs[0].shape[1] - LANES
    width = features // peers

    def stacked(columns):
        return jnp.concatenate([ref[:, columns] for ref in in_refs], axis=0)

    def columns_of(k):
        return stacked(pl.ds(pl.multiple_of((me ^ k) * width, LANES), width))

    band = stacked(slice(0, BAND))
    flag = stacked(slice(features, features + LANES))
    for ref, pieces in zip(out_refs, [[0], [1]] + [[k, k + 1] for k in range(2, peers, 2)]):
        for i, k in enumerate(pieces):
            ref[:, i * width : (i + 1) * width] = columns_of(k)
        end = len(pieces) * width
        ref[:, end : end + BAND] = band
        ref[:, end + BAND :] = flag


def finish_kernel(*refs):
    row_refs, (sum_ref, routed_ref, shared_ref, routed, sems) = refs[:-5], refs[-5:]
    _, band_size, width = routed_ref.shape
    copies = []

    def send(source, target):
        copies.append(pltpu.make_async_copy(source, target, sems.at[len(copies)]))
        copies[-1].start()

    def tail(ref, start, size):
        start += ref.shape[1] - BAND - LANES
        return ref[:, start : start + size]

    rows = jnp.concatenate([ref[:, :width] for ref in row_refs], axis=0)
    band = jnp.concatenate([tail(ref, 0, BAND) for ref in row_refs], axis=0)
    count = sum(
        jnp.sum(tail(ref, BAND, LANES).astype(jnp.float32), axis=0, keepdims=True)[:, :1]
        for ref in row_refs
    )
    for begin in range(0, band_size, LANES):
        part = slice(begin, begin + LANES)
        product = lax.dot_general(
            band[:, part], rows, (((0,), (0,)), ((), ())), preferred_element_type=jnp.float32
        )
        routed[part] = product * (2.0 / count)
        send(routed.at[part], routed_ref.at[0, part])
    send(sum_ref, shared_ref)
    for copy in copies:
        copy.wait()


def select(ids, expert):
    tokens = ids.shape[1]
    member = jnp.max((ids == expert).astype(jnp.float32), axis=0, keepdims=True)
    earlier = (
        lax.broadcasted_iota(jnp.int32, (tokens, tokens), 0)
        < lax.broadcasted_iota(jnp.int32, (tokens, tokens), 1)
    ).astype(jnp.bfloat16)
    rank = jnp.dot(member.astype(jnp.bfloat16), earlier, preferred_element_type=jnp.float32)
    slot = lax.broadcasted_iota(jnp.int32, (2 * CAP, tokens), 0).astype(jnp.float32)
    return jnp.where(slot == rank, member, 0.0)


def fetch_kernel(ids_ref, tokens_ref, held_ids_ref, held_ref, sems):
    copies = [
        pltpu.make_async_copy(ids_ref, held_ids_ref, sems.at[0]),
        pltpu.make_async_copy(tokens_ref, held_ref, sems.at[1]),
    ]
    for copy in copies:
        copy.start()
    for copy in copies:
        copy.wait()


def pair_kernel(
    ids_ref, other_ids_ref, mine_ref, other_ref, *out_refs, experts, peers, wanted, aligned
):
    out_refs, row_refs = out_refs[: -experts // 2], out_refs[-experts // 2 :]
    features = mine_ref.shape[1]
    e = lax.axis_index("expert")
    d = lax.axis_index("dp")

    def both(columns):
        return jnp.concatenate([mine_ref[:, columns], other_ref[:, columns]], axis=0)

    lead = both(slice(0, SBAND))

    def product(columns):
        return lax.dot_general(
            both(columns), lead, (((0,), (0,)), ((), ())), preferred_element_type=jnp.float32
        )

    if aligned:
        share = features // (experts * peers)
        half = LANES // 2
        window = share + half * (share // half % 2)
        for out_ref, pairs in zip(out_refs, wanted):
            for i, (m, k) in enumerate(pairs):
                start = ((e ^ m) * peers + (d ^ k)) * (share // half)
                odd = start % 2
                found = product(pl.ds(pl.multiple_of((start - odd) * half, LANES), window))
                if window > share:
                    found = jnp.where(odd == 1, found[half:], found[:share])
                out_ref[i * share : (i + 1) * share] = found
            filled = len(pairs) * share
            if out_ref.shape[0] > filled:
                out_ref[filled:] = jnp.zeros_like(out_ref[filled:])
    else:
        for part in parts_of(features):
            out_refs[0][part] = product(part)

    ids = jnp.concatenate([ids_ref[...], other_ids_ref[...]], axis=1)
    picks = jnp.concatenate(
        [select(ids, e ^ (k + d % 2)) for k in range(0, experts, 2)], axis=0
    )
    flags = jnp.broadcast_to(jnp.sum(picks, axis=1, keepdims=True), (picks.shape[0], LANES))
    picks = picks.astype(jnp.bfloat16)
    for part in parts_of(features):
        chosen = jnp.dot(picks, both(part), preferred_element_type=jnp.float32)
        for i, ref in enumerate(row_refs):
            ref[:, part] = chosen[2 * CAP * i : 2 * CAP * (i + 1)].astype(jnp.bfloat16)
    for i, ref in enumerate(row_refs):
        ref[:, features:] = flags[2 * CAP * i : 2 * CAP * (i + 1)].astype(jnp.bfloat16)


def on_device(tokens, expert_ids):
    tok_rows, features = tokens.shape
    experts = lax.axis_size("expert")
    peers = lax.axis_size("dp")
    width = features // peers
    share = features // (experts * peers)
    anywhere = pl.BlockSpec(memory_space=pl.ANY)
    inside = pl.BlockSpec(memory_space=pltpu.VMEM)

    ids = expert_ids.T
    other = exchange(tokens, "dp", 1)
    other_ids = exchange(ids, "dp", 1)
    ids, mine = call(
        fetch_kernel,
        [
            jax.ShapeDtypeStruct(ids.shape, ids.dtype),
            jax.ShapeDtypeStruct(tokens.shape, tokens.dtype),
        ],
        ids,
        tokens,
        flops=0,
        nbytes=4 * tok_rows * features,
        in_specs=[anywhere, anywhere],
        out_specs=[inside, inside],
        scratch_shapes=[pltpu.SemaphoreType.DMA((2,))],
    )
    ids, mine, other, other_ids = lax.optimization_barrier((ids, mine, other, other_ids))

    even = range(0, peers, 2)
    far = range(2, experts, 2)
    groups = [[m + 1 for m in far], [*far], [1], [0]]
    wanted = [[(m, k) for m in group] for group in groups for k in even]
    aligned = share % (LANES // 2) == 0
    sizes = [len(pairs) * share for pairs in wanted]
    for i in range(1, peers // 2):
        sizes[i] += PAD
    found = call(
        functools.partial(
            pair_kernel, experts=experts, peers=peers, wanted=wanted, aligned=aligned
        ),
        [
            jax.ShapeDtypeStruct((size, SBAND), jnp.float32)
            for size in (sizes if aligned else [features])
        ]
        + [jax.ShapeDtypeStruct((2 * CAP, features + LANES), jnp.bfloat16)] * (experts // 2),
        ids,
        other_ids,
        mine,
        other,
        flops=4 * tok_rows * features * (SBAND + experts * CAP),
        nbytes=4 * tok_rows * features + 4 * features * SBAND,
    )
    blocks, outgoing = found[: -experts // 2], found[-experts // 2 :]
    if not aligned:
        e, d = lax.axis_index("expert"), lax.axis_index("dp")
        blocks = [
            jnp.concatenate(
                [
                    lax.dynamic_slice_in_dim(
                        blocks[0], ((e ^ m) * peers + (d ^ k)) * share, share, axis=0
                    )
                    for m, k in pairs
                ],
                axis=0,
            )
            for pairs in wanted
        ]
    def over_dp(i, after=None):
        own, *sent = blocks[i * (peers // 2) : (i + 1) * (peers // 2)]
        got = [exchange(tie(x, after), "dp", 2 * k + 2) for k, x in enumerate(sent)]
        return sum([x[: own.shape[0]] for x in got], own)

    odd = over_dp(0)
    near = exchange(odd, "expert", 1)
    paired = over_dp(1, odd) + near
    beside_sum = exchange(over_dp(2), "expert", 1)
    own = over_dp(3, near) + beside_sum

    arrived = [pass_on(outgoing[k], 2 * k) for k in range(experts // 2)]
    arrived[0] = jnp.where(lax.axis_index("dp") % 2 == 0, outgoing[0], arrived[0])

    rows = experts * CAP
    tail = BAND + LANES
    mine, give, *packed = call(
        functools.partial(split_kernel, peers=peers),
        [jax.ShapeDtypeStruct((rows, width + tail), jnp.bfloat16)] * 2
        + [jax.ShapeDtypeStruct((rows, 2 * width + tail), jnp.bfloat16)] * (peers // 2 - 1),
        *arrived,
        flops=0,
        nbytes=4 * rows * features,
    )
    across = [exchange(x, "dp", 2 * k + 2) for k, x in enumerate(packed)]
    beside = exchange(jnp.concatenate([give] + [x[:, width:] for x in across]), "dp", 1)
    gathered = [mine, *across, beside]
    paired = tie(paired, packed)
    others = [
        exchange(paired[i * share : (i + 1) * share], "expert", m) for i, m in enumerate(far)
    ]
    summed = sum(others, lax.optimization_barrier(own))
    shared_out = summed * (2.0 / (tok_rows * experts * peers))
    routed_out, shared_out = call(
        finish_kernel,
        [
            jax.ShapeDtypeStruct((1, BAND, width), jnp.float32),
            jax.ShapeDtypeStruct((share, SBAND), jnp.float32),
        ],
        *gathered,
        shared_out,
        flops=2 * BAND * width * rows * peers,
        nbytes=4 * BAND * width,
        in_specs=[inside] * (len(gathered) + 1),
        out_specs=[anywhere, anywhere],
        scratch_shapes=[
            pltpu.VMEM((BAND, width), jnp.float32),
            pltpu.SemaphoreType.DMA((BAND // LANES + 1,)),
        ],
    )
    return routed_out, shared_out


def solution(mesh):
    in_specs = (P(("groups", "expert", "dp"), None), P(("groups", "expert", "dp"), None))
    out_specs = (P(("groups", "expert"), None, "dp"), P(("groups", "expert", "dp"), None))
    return jax.shard_map(
        on_device, mesh=mesh, in_specs=in_specs, out_specs=out_specs, check_vma=False
    )
```

```python
import functools

import jax
import jax.numpy as jnp
from jax import lax
from jax.experimental import pallas as pl
from jax.experimental.pallas import tpu as pltpu
from jax.sharding import PartitionSpec as P

BAND = 384
SBAND = 128
CAP = 8
LANES = 128
PAD = 16
VMEM_LIMIT = 16 * 1024 * 1024


def exchange(value, axis, distance):
    size = lax.axis_size(axis)
    return lax.ppermute(value, axis, [(i, i ^ distance) for i in range(size)])


def tie(value, after):
    return value if after is None else lax.optimization_barrier((value, after))[0]


def pass_on(value, distance):
    experts, peers = lax.axis_size("expert"), lax.axis_size("dp")
    pairs = [
        (e * peers + d, (e ^ (distance + d % 2)) * peers + d)
        for e in range(experts)
        for d in range(peers)
        if distance + d % 2
    ]
    return lax.ppermute(value, ("expert", "dp"), pairs)


def call(kernel, out_shape, *operands, flops, nbytes, **where):
    return pl.pallas_call(
        kernel,
        out_shape=out_shape,
        compiler_params=pltpu.CompilerParams(vmem_limit_bytes=VMEM_LIMIT),
        cost_estimate=pl.CostEstimate(flops=flops, bytes_accessed=nbytes, transcendentals=0),
        **where,
    )(*operands)


def parts_of(features):
    step = -(-features // (4 * LANES)) * LANES
    return [slice(b, min(b + step, features)) for b in range(0, features, step)]


def split_kernel(*refs, peers):
    in_refs, out_refs = refs[: -1 - peers // 2], refs[-1 - peers // 2 :]
    me = lax.axis_index("dp")
    features = in_refs[0].shape[1] - LANES
    width = features // peers

    def stacked(columns):
        return jnp.concatenate([ref[:, columns] for ref in in_refs], axis=0)

    def columns_of(k):
        return stacked(pl.ds(pl.multiple_of((me ^ k) * width, LANES), width))

    band = stacked(slice(0, BAND))
    flag = stacked(slice(features, features + LANES))
    for ref, pieces in zip(out_refs, [[0], [1]] + [[k, k + 1] for k in range(2, peers, 2)]):
        for i, k in enumerate(pieces):
            ref[:, i * width : (i + 1) * width] = columns_of(k)
        end = len(pieces) * width
        ref[:, end : end + BAND] = band
        ref[:, end + BAND :] = flag


def finish_kernel(*refs):
    row_refs, (sum_ref, routed_ref, shared_ref, routed, sems) = refs[:-5], refs[-5:]
    _, band_size, width = routed_ref.shape
    copies = []

    def send(source, target):
        copies.append(pltpu.make_async_copy(source, target, sems.at[len(copies)]))
        copies[-1].start()

    def tail(ref, start, size):
        start += ref.shape[1] - BAND - LANES
        return ref[:, start : start + size]

    rows = jnp.concatenate([ref[:, :width] for ref in row_refs], axis=0)
    band = jnp.concatenate([tail(ref, 0, BAND) for ref in row_refs], axis=0)
    count = sum(
        jnp.sum(tail(ref, BAND, LANES).astype(jnp.float32), axis=0, keepdims=True)[:, :1]
        for ref in row_refs
    )
    for begin in range(0, band_size, LANES):
        part = slice(begin, begin + LANES)
        product = lax.dot_general(
            band[:, part], rows, (((0,), (0,)), ((), ())), preferred_element_type=jnp.float32
        )
        routed[part] = product * (2.0 / count)
        send(routed.at[part], routed_ref.at[0, part])
    send(sum_ref, shared_ref)
    for copy in copies:
        copy.wait()


def select(ids, expert):
    tokens = ids.shape[1]
    member = jnp.max((ids == expert).astype(jnp.float32), axis=0, keepdims=True)
    earlier = (
        lax.broadcasted_iota(jnp.int32, (tokens, tokens), 0)
        < lax.broadcasted_iota(jnp.int32, (tokens, tokens), 1)
    ).astype(jnp.bfloat16)
    rank = jnp.dot(member.astype(jnp.bfloat16), earlier, preferred_element_type=jnp.float32)
    slot = lax.broadcasted_iota(jnp.int32, (CAP, tokens), 0).astype(jnp.float32)
    return jnp.where(slot == rank, member, 0.0)


def picks_of(ids_ref, experts):
    e, d = lax.axis_index("expert"), lax.axis_index("dp")
    picks = [select(ids_ref[...], e ^ (k + d % 2)) for k in range(0, experts, 2)]
    picks = jnp.concatenate(picks, axis=0)
    flags = jnp.broadcast_to(jnp.sum(picks, axis=1, keepdims=True), (picks.shape[0], LANES))
    return picks.astype(jnp.bfloat16), flags


def fetch_kernel(ids_ref, tokens_ref, held_ref, rows_ref, sems):
    features = tokens_ref.shape[1]
    parts = parts_of(features)
    copies = [
        pltpu.make_async_copy(tokens_ref.at[:, part], held_ref.at[:, part], sems.at[i])
        for i, part in enumerate(parts)
    ]
    for copy in copies:
        copy.start()
    picks, flags = picks_of(ids_ref, 2 * rows_ref.shape[0] // CAP)
    rows_ref[:, features:] = flags
    for copy, part in zip(copies, parts):
        copy.wait()
        rows_ref[:, part] = jnp.dot(
            picks, held_ref[:, part], preferred_element_type=jnp.float32
        )


def pair_kernel(
    other_ids_ref, rows_ref, mine_ref, other_ref, *out_refs, experts, peers, wanted, aligned
):
    out_refs, row_refs = out_refs[: -experts // 2], out_refs[-experts // 2 :]
    features = mine_ref.shape[1]
    e = lax.axis_index("expert")
    d = lax.axis_index("dp")

    def both(columns):
        return jnp.concatenate([mine_ref[:, columns], other_ref[:, columns]], axis=0)

    lead = both(slice(0, SBAND))

    def product(columns):
        return lax.dot_general(
            both(columns), lead, (((0,), (0,)), ((), ())), preferred_element_type=jnp.float32
        )

    if aligned:
        share = features // (experts * peers)
        half = LANES // 2
        window = share + half * (share // half % 2)
        for out_ref, pairs in zip(out_refs, wanted):
            for i, (m, k) in enumerate(pairs):
                start = ((e ^ m) * peers + (d ^ k)) * (share // half)
                odd = start % 2
                found = product(pl.ds(pl.multiple_of((start - odd) * half, LANES), window))
                if window > share:
                    found = jnp.where(odd == 1, found[half:], found[:share])
                out_ref[i * share : (i + 1) * share] = found
            filled = len(pairs) * share
            if out_ref.shape[0] > filled:
                out_ref[filled:] = jnp.zeros_like(out_ref[filled:])
    else:
        for part in parts_of(features):
            out_refs[0][part] = product(part)

    picks, flags = picks_of(other_ids_ref, experts)

    def put(columns, found):
        for i, ref in enumerate(row_refs):
            part = slice(i * CAP, (i + 1) * CAP)
            both_rows = jnp.concatenate([rows_ref[part, columns], found[part]], axis=0)
            ref[:, columns] = both_rows.astype(jnp.bfloat16)

    for part in parts_of(features):
        put(part, jnp.dot(picks, other_ref[:, part], preferred_element_type=jnp.float32))
    put(slice(features, features + LANES), flags)


def on_device(tokens, expert_ids):
    tok_rows, features = tokens.shape
    experts = lax.axis_size("expert")
    peers = lax.axis_size("dp")
    width = features // peers
    share = features // (experts * peers)
    anywhere = pl.BlockSpec(memory_space=pl.ANY)
    inside = pl.BlockSpec(memory_space=pltpu.VMEM)

    ids = expert_ids.T
    other = exchange(tokens, "dp", 1)
    other_ids = exchange(ids, "dp", 1)
    mine, own_rows = call(
        fetch_kernel,
        [
            jax.ShapeDtypeStruct(tokens.shape, tokens.dtype),
            jax.ShapeDtypeStruct((experts * CAP // 2, features + LANES), jnp.float32),
        ],
        ids,
        tokens,
        flops=0,
        nbytes=4 * tok_rows * features,
        in_specs=[inside, anywhere],
        out_specs=[inside, inside],
        scratch_shapes=[pltpu.SemaphoreType.DMA((len(parts_of(features)),))],
    )
    own_rows, mine, other, other_ids = lax.optimization_barrier(
        (own_rows, mine, other, other_ids)
    )

    even = range(0, peers, 2)
    far = range(2, experts, 2)
    groups = [[m + 1 for m in far], [*far], [1], [0]]
    wanted = [[(m, k) for m in group] for group in groups for k in even]
    aligned = share % (LANES // 2) == 0
    sizes = [len(pairs) * share for pairs in wanted]
    for i in range(1, peers // 2):
        sizes[i] += PAD
    found = call(
        functools.partial(
            pair_kernel, experts=experts, peers=peers, wanted=wanted, aligned=aligned
        ),
        [
            jax.ShapeDtypeStruct((size, SBAND), jnp.float32)
            for size in (sizes if aligned else [features])
        ]
        + [jax.ShapeDtypeStruct((2 * CAP, features + LANES), jnp.bfloat16)] * (experts // 2),
        other_ids,
        own_rows,
        mine,
        other,
        flops=4 * tok_rows * features * (SBAND + experts * CAP),
        nbytes=4 * tok_rows * features + 4 * features * SBAND,
    )
    blocks, outgoing = found[: -experts // 2], found[-experts // 2 :]
    if not aligned:
        e, d = lax.axis_index("expert"), lax.axis_index("dp")
        blocks = [
            jnp.concatenate(
                [
                    lax.dynamic_slice_in_dim(
                        blocks[0], ((e ^ m) * peers + (d ^ k)) * share, share, axis=0
                    )
                    for m, k in pairs
                ],
                axis=0,
            )
            for pairs in wanted
        ]
    def over_dp(i, after=None):
        own, *sent = blocks[i * (peers // 2) : (i + 1) * (peers // 2)]
        got = [exchange(tie(x, after), "dp", 2 * k + 2) for k, x in enumerate(sent)]
        return sum([x[: own.shape[0]] for x in got], own)

    odd = over_dp(0)
    near = exchange(odd, "expert", 1)
    paired = over_dp(1, odd) + near
    beside_sum = exchange(over_dp(2), "expert", 1)
    own = over_dp(3, near) + beside_sum

    arrived = [pass_on(outgoing[k], 2 * k) for k in range(experts // 2)]
    arrived[0] = jnp.where(lax.axis_index("dp") % 2 == 0, outgoing[0], arrived[0])

    rows = experts * CAP
    tail = BAND + LANES
    mine, give, *packed = call(
        functools.partial(split_kernel, peers=peers),
        [jax.ShapeDtypeStruct((rows, width + tail), jnp.bfloat16)] * 2
        + [jax.ShapeDtypeStruct((rows, 2 * width + tail), jnp.bfloat16)] * (peers // 2 - 1),
        *arrived,
        flops=0,
        nbytes=4 * rows * features,
    )
    across = [exchange(x, "dp", 2 * k + 2) for k, x in enumerate(packed)]
    beside = exchange(jnp.concatenate([give] + [x[:, width:] for x in across]), "dp", 1)
    gathered = [mine, *across, beside]
    paired = tie(paired, packed)
    others = [
        exchange(paired[i * share : (i + 1) * share], "expert", m) for i, m in enumerate(far)
    ]
    summed = sum(others, lax.optimization_barrier(own))
    shared_out = summed * (2.0 / (tok_rows * experts * peers))
    routed_out, shared_out = call(
        finish_kernel,
        [
            jax.ShapeDtypeStruct((1, BAND, width), jnp.float32),
            jax.ShapeDtypeStruct((share, SBAND), jnp.float32),
        ],
        *gathered,
        shared_out,
        flops=2 * BAND * width * rows * peers,
        nbytes=4 * BAND * width,
        in_specs=[inside] * (len(gathered) + 1),
        out_specs=[anywhere, anywhere],
        scratch_shapes=[
            pltpu.VMEM((BAND, width), jnp.float32),
            pltpu.SemaphoreType.DMA((BAND // LANES + 1,)),
        ],
    )
    return routed_out, shared_out


def solution(mesh):
    in_specs = (P(("groups", "expert", "dp"), None), P(("groups", "expert", "dp"), None))
    out_specs = (P(("groups", "expert"), None, "dp"), P(("groups", "expert", "dp"), None))
    return jax.shard_map(
        on_device, mesh=mesh, in_specs=in_specs, out_specs=out_specs, check_vma=False
    )
```

```python
import functools

import jax
import jax.numpy as jnp
from jax import lax
from jax.experimental import pallas as pl
from jax.experimental.pallas import tpu as pltpu
from jax.sharding import PartitionSpec as P

BAND = 384
SBAND = 128
CAP = 8
LANES = 128
PAD = 16
VMEM_LIMIT = 16 * 1024 * 1024


def exchange(value, axis, distance):
    size = lax.axis_size(axis)
    return lax.ppermute(value, axis, [(i, i ^ distance) for i in range(size)])


def tie(value, after):
    return value if after is None else lax.optimization_barrier((value, after))[0]


def pass_on(value, distance):
    experts, peers = lax.axis_size("expert"), lax.axis_size("dp")
    pairs = [
        (e * peers + d, (e ^ (distance + d % 2)) * peers + d)
        for e in range(experts)
        for d in range(peers)
        if distance + d % 2
    ]
    return lax.ppermute(value, ("expert", "dp"), pairs)


def call(kernel, out_shape, *operands, flops, nbytes, **where):
    return pl.pallas_call(
        kernel,
        out_shape=out_shape,
        compiler_params=pltpu.CompilerParams(vmem_limit_bytes=VMEM_LIMIT),
        cost_estimate=pl.CostEstimate(flops=flops, bytes_accessed=nbytes, transcendentals=0),
        **where,
    )(*operands)


def parts_of(features):
    step = -(-features // (4 * LANES)) * LANES
    return [slice(b, min(b + step, features)) for b in range(0, features, step)]


def split_kernel(*refs, peers):
    in_refs, out_refs = refs[: -1 - peers // 2], refs[-1 - peers // 2 :]
    me = lax.axis_index("dp")
    features = in_refs[0].shape[1] - LANES
    width = features // peers

    def stacked(columns):
        return jnp.concatenate([ref[:, columns] for ref in in_refs], axis=0)

    def columns_of(k):
        return stacked(pl.ds(pl.multiple_of((me ^ k) * width, LANES), width))

    band = stacked(slice(0, BAND))
    flag = stacked(slice(features, features + LANES))
    for ref, pieces in zip(out_refs, [[0], [1]] + [[k, k + 1] for k in range(2, peers, 2)]):
        for i, k in enumerate(pieces):
            ref[:, i * width : (i + 1) * width] = columns_of(k)
        end = len(pieces) * width
        ref[:, end : end + BAND] = band
        ref[:, end + BAND :] = flag


def finish_kernel(*refs):
    row_refs, (sum_ref, routed_ref, shared_ref, routed, sems) = refs[:-5], refs[-5:]
    _, band_size, width = routed_ref.shape
    copies = []

    def send(source, target):
        copies.append(pltpu.make_async_copy(source, target, sems.at[len(copies)]))
        copies[-1].start()

    def tail(ref, start, size):
        start += ref.shape[1] - BAND - LANES
        return ref[:, start : start + size]

    send(sum_ref, shared_ref)
    rows = jnp.concatenate([ref[:, :width] for ref in row_refs], axis=0)
    band = jnp.concatenate([tail(ref, 0, BAND) for ref in row_refs], axis=0)
    count = sum(
        jnp.sum(tail(ref, BAND, LANES).astype(jnp.float32), axis=0, keepdims=True)[:, :1]
        for ref in row_refs
    )
    for begin in range(0, band_size, LANES):
        part = slice(begin, begin + LANES)
        product = lax.dot_general(
            band[:, part], rows, (((0,), (0,)), ((), ())), preferred_element_type=jnp.float32
        )
        routed[part] = product * (2.0 / count)
        send(routed.at[part], routed_ref.at[0, part])
    for copy in copies:
        copy.wait()


def select(ids, expert):
    tokens = ids.shape[1]
    member = jnp.max((ids == expert).astype(jnp.float32), axis=0, keepdims=True)
    earlier = (
        lax.broadcasted_iota(jnp.int32, (tokens, tokens), 0)
        < lax.broadcasted_iota(jnp.int32, (tokens, tokens), 1)
    ).astype(jnp.bfloat16)
    rank = jnp.dot(member.astype(jnp.bfloat16), earlier, preferred_element_type=jnp.float32)
    slot = lax.broadcasted_iota(jnp.int32, (CAP, tokens), 0).astype(jnp.float32)
    return jnp.where(slot == rank, member, 0.0)


def picks_of(ids_ref, experts):
    e, d = lax.axis_index("expert"), lax.axis_index("dp")
    picks = [select(ids_ref[...], e ^ (k + d % 2)) for k in range(0, experts, 2)]
    picks = jnp.concatenate(picks, axis=0)
    flags = jnp.broadcast_to(jnp.sum(picks, axis=1, keepdims=True), (picks.shape[0], LANES))
    return picks.astype(jnp.bfloat16), flags


def fetch_kernel(ids_ref, tokens_ref, held_ref, rows_ref, sems):
    features = tokens_ref.shape[1]
    parts = parts_of(features)
    copies = [
        pltpu.make_async_copy(tokens_ref.at[:, part], held_ref.at[:, part], sems.at[i])
        for i, part in enumerate(parts)
    ]
    for copy in copies:
        copy.start()
    picks, flags = picks_of(ids_ref, 2 * rows_ref.shape[0] // CAP)
    rows_ref[:, features:] = flags
    for copy, part in zip(copies, parts):
        copy.wait()
        rows_ref[:, part] = jnp.dot(
            picks, held_ref[:, part], preferred_element_type=jnp.float32
        )


def pair_kernel(
    other_ids_ref, rows_ref, mine_ref, other_ref, *out_refs, experts, peers, wanted, aligned
):
    out_refs, row_refs = out_refs[: -experts // 2], out_refs[-experts // 2 :]
    features = mine_ref.shape[1]
    e = lax.axis_index("expert")
    d = lax.axis_index("dp")

    def both(columns):
        return jnp.concatenate([mine_ref[:, columns], other_ref[:, columns]], axis=0)

    lead = both(slice(0, SBAND))

    def product(columns):
        return lax.dot_general(
            both(columns), lead, (((0,), (0,)), ((), ())), preferred_element_type=jnp.float32
        )

    if aligned:
        share = features // (experts * peers)
        half = LANES // 2
        window = share + half * (share // half % 2)
        for out_ref, pairs in zip(out_refs, wanted):
            for i, (m, k) in enumerate(pairs):
                start = ((e ^ m) * peers + (d ^ k)) * (share // half)
                odd = start % 2
                found = product(pl.ds(pl.multiple_of((start - odd) * half, LANES), window))
                if window > share:
                    found = jnp.where(odd == 1, found[half:], found[:share])
                out_ref[i * share : (i + 1) * share] = found
            filled = len(pairs) * share
            if out_ref.shape[0] > filled:
                out_ref[filled:] = jnp.zeros_like(out_ref[filled:])
    else:
        for part in parts_of(features):
            out_refs[0][part] = product(part)

    picks, flags = picks_of(other_ids_ref, experts)

    def put(columns, found):
        for i, ref in enumerate(row_refs):
            part = slice(i * CAP, (i + 1) * CAP)
            both_rows = jnp.concatenate([rows_ref[part, columns], found[part]], axis=0)
            ref[:, columns] = both_rows.astype(jnp.bfloat16)

    for part in parts_of(features):
        put(part, jnp.dot(picks, other_ref[:, part], preferred_element_type=jnp.float32))
    put(slice(features, features + LANES), flags)


def on_device(tokens, expert_ids):
    tok_rows, features = tokens.shape
    experts = lax.axis_size("expert")
    peers = lax.axis_size("dp")
    width = features // peers
    share = features // (experts * peers)
    anywhere = pl.BlockSpec(memory_space=pl.ANY)
    inside = pl.BlockSpec(memory_space=pltpu.VMEM)

    ids = expert_ids.T
    other = exchange(tokens, "dp", 1)
    other_ids = exchange(ids, "dp", 1)
    mine, own_rows = call(
        fetch_kernel,
        [
            jax.ShapeDtypeStruct(tokens.shape, tokens.dtype),
            jax.ShapeDtypeStruct((experts * CAP // 2, features + LANES), jnp.float32),
        ],
        ids,
        tokens,
        flops=0,
        nbytes=4 * tok_rows * features,
        in_specs=[inside, anywhere],
        out_specs=[inside, inside],
        scratch_shapes=[pltpu.SemaphoreType.DMA((len(parts_of(features)),))],
    )
    own_rows, mine, other, other_ids = lax.optimization_barrier(
        (own_rows, mine, other, other_ids)
    )

    even = range(0, peers, 2)
    far = range(2, experts, 2)
    groups = [[m + 1 for m in far], [*far], [1], [0]]
    wanted = [[(m, k) for m in group] for group in groups for k in even]
    aligned = share % (LANES // 2) == 0
    sizes = [len(pairs) * share for pairs in wanted]
    for i in range(1, peers // 2):
        sizes[i] += PAD
    found = call(
        functools.partial(
            pair_kernel, experts=experts, peers=peers, wanted=wanted, aligned=aligned
        ),
        [
            jax.ShapeDtypeStruct((size, SBAND), jnp.float32)
            for size in (sizes if aligned else [features])
        ]
        + [jax.ShapeDtypeStruct((2 * CAP, features + LANES), jnp.bfloat16)] * (experts // 2),
        other_ids,
        own_rows,
        mine,
        other,
        flops=4 * tok_rows * features * (SBAND + experts * CAP),
        nbytes=4 * tok_rows * features + 4 * features * SBAND,
    )
    blocks, outgoing = found[: -experts // 2], found[-experts // 2 :]
    if not aligned:
        e, d = lax.axis_index("expert"), lax.axis_index("dp")
        blocks = [
            jnp.concatenate(
                [
                    lax.dynamic_slice_in_dim(
                        blocks[0], ((e ^ m) * peers + (d ^ k)) * share, share, axis=0
                    )
                    for m, k in pairs
                ],
                axis=0,
            )
            for pairs in wanted
        ]
    def over_dp(i, after=None):
        own, *sent = blocks[i * (peers // 2) : (i + 1) * (peers // 2)]
        got = [exchange(tie(x, after), "dp", 2 * k + 2) for k, x in enumerate(sent)]
        return sum([x[: own.shape[0]] for x in got], own)

    odd = over_dp(0)
    near = exchange(odd, "expert", 1)
    paired = over_dp(1, odd) + near
    beside_sum = exchange(over_dp(2), "expert", 1)
    own = over_dp(3, near) + beside_sum

    arrived = [pass_on(outgoing[k], 2 * k) for k in range(experts // 2)]
    arrived[0] = jnp.where(lax.axis_index("dp") % 2 == 0, outgoing[0], arrived[0])

    rows = experts * CAP
    tail = BAND + LANES
    mine, give, *packed = call(
        functools.partial(split_kernel, peers=peers),
        [jax.ShapeDtypeStruct((rows, width + tail), jnp.bfloat16)] * 2
        + [jax.ShapeDtypeStruct((rows, 2 * width + tail), jnp.bfloat16)] * (peers // 2 - 1),
        *arrived,
        flops=0,
        nbytes=4 * rows * features,
    )
    across = [exchange(x, "dp", 2 * k + 2) for k, x in enumerate(packed)]
    beside = exchange(jnp.concatenate([give] + [x[:, width:] for x in across]), "dp", 1)
    gathered = [mine, *across, beside]
    paired = tie(paired, packed)
    others = [
        exchange(paired[i * share : (i + 1) * share], "expert", m) for i, m in enumerate(far)
    ]
    summed = sum(others, lax.optimization_barrier(own))
    shared_out = summed * (2.0 / (tok_rows * experts * peers))
    routed_out, shared_out = call(
        finish_kernel,
        [
            jax.ShapeDtypeStruct((1, BAND, width), jnp.float32),
            jax.ShapeDtypeStruct((share, SBAND), jnp.float32),
        ],
        *gathered,
        shared_out,
        flops=2 * BAND * width * rows * peers,
        nbytes=4 * BAND * width,
        in_specs=[inside] * (len(gathered) + 1),
        out_specs=[anywhere, anywhere],
        scratch_shapes=[
            pltpu.VMEM((BAND, width), jnp.float32),
            pltpu.SemaphoreType.DMA((BAND // LANES + 1,)),
        ],
    )
    return routed_out, shared_out


def solution(mesh):
    in_specs = (P(("groups", "expert", "dp"), None), P(("groups", "expert", "dp"), None))
    out_specs = (P(("groups", "expert"), None, "dp"), P(("groups", "expert", "dp"), None))
    return jax.shard_map(
        on_device, mesh=mesh, in_specs=in_specs, out_specs=out_specs, check_vma=False
    )
```

```python
import functools

import jax
import jax.numpy as jnp
from jax import lax
from jax.experimental import pallas as pl
from jax.experimental.pallas import tpu as pltpu
from jax.sharding import PartitionSpec as P

BAND = 384
SBAND = 128
CAP = 8
LANES = 128
PAD = 16
VMEM_LIMIT = 16 * 1024 * 1024


def exchange(value, axis, distance):
    size = lax.axis_size(axis)
    return lax.ppermute(value, axis, [(i, i ^ distance) for i in range(size)])


def tie(value, after):
    return value if after is None else lax.optimization_barrier((value, after))[0]


def pass_on(value, distance):
    experts, peers = lax.axis_size("expert"), lax.axis_size("dp")
    pairs = [
        (e * peers + d, (e ^ (distance + d % 2)) * peers + d)
        for e in range(experts)
        for d in range(peers)
        if distance + d % 2
    ]
    return lax.ppermute(value, ("expert", "dp"), pairs)


def call(kernel, out_shape, *operands, flops, nbytes, **where):
    return pl.pallas_call(
        kernel,
        out_shape=out_shape,
        compiler_params=pltpu.CompilerParams(vmem_limit_bytes=VMEM_LIMIT),
        cost_estimate=pl.CostEstimate(flops=flops, bytes_accessed=nbytes, transcendentals=0),
        **where,
    )(*operands)


def parts_of(features):
    step = -(-features // (4 * LANES)) * LANES
    return [slice(b, min(b + step, features)) for b in range(0, features, step)]


def split_kernel(*refs, peers):
    in_refs, out_refs = refs[: -1 - peers // 2], refs[-1 - peers // 2 :]
    me = lax.axis_index("dp")
    features = in_refs[0].shape[1] - LANES
    width = features // peers

    def stacked(columns):
        return jnp.concatenate([ref[:, columns] for ref in in_refs], axis=0)

    def columns_of(k):
        return stacked(pl.ds(pl.multiple_of((me ^ k) * width, LANES), width))

    band = stacked(slice(0, BAND))
    flag = stacked(slice(features, features + LANES))
    for ref, pieces in zip(out_refs, [[0], [1]] + [[k, k + 1] for k in range(2, peers, 2)]):
        for i, k in enumerate(pieces):
            ref[:, i * width : (i + 1) * width] = columns_of(k)
        end = len(pieces) * width
        ref[:, end : end + BAND] = band
        ref[:, end + BAND :] = flag


def finish_kernel(*refs):
    row_refs, (sum_ref, routed_ref, shared_ref, routed, sems) = refs[:-5], refs[-5:]
    _, band_size, width = routed_ref.shape
    copies = []

    def send(source, target):
        copies.append(pltpu.make_async_copy(source, target, sems.at[len(copies)]))
        copies[-1].start()

    def tail(ref, start, size):
        start += ref.shape[1] - BAND - LANES
        return ref[:, start : start + size]

    send(sum_ref, shared_ref)
    rows = jnp.concatenate([ref[:, :width] for ref in row_refs], axis=0)
    band = jnp.concatenate([tail(ref, 0, BAND) for ref in row_refs], axis=0)
    count = sum(
        jnp.sum(tail(ref, BAND, LANES).astype(jnp.float32), axis=0, keepdims=True)[:, :1]
        for ref in row_refs
    )
    for begin in range(0, band_size, LANES):
        part = slice(begin, begin + LANES)
        product = lax.dot_general(
            band[:, part], rows, (((0,), (0,)), ((), ())), preferred_element_type=jnp.float32
        )
        routed[part] = product * (2.0 / count)
        send(routed.at[part], routed_ref.at[0, part])
    for copy in copies:
        copy.wait()


def select(ids, expert):
    tokens = ids.shape[1]
    member = jnp.max((ids == expert).astype(jnp.float32), axis=0, keepdims=True)
    earlier = (
        lax.broadcasted_iota(jnp.int32, (tokens, tokens), 0)
        < lax.broadcasted_iota(jnp.int32, (tokens, tokens), 1)
    ).astype(jnp.bfloat16)
    rank = jnp.dot(member.astype(jnp.bfloat16), earlier, preferred_element_type=jnp.float32)
    slot = lax.broadcasted_iota(jnp.int32, (CAP, tokens), 0).astype(jnp.float32)
    return jnp.where(slot == rank, member, 0.0)


def picks_of(ids_ref, experts):
    e, d = lax.axis_index("expert"), lax.axis_index("dp")
    picks = [select(ids_ref[...], e ^ (k + d % 2)) for k in range(0, experts, 2)]
    picks = jnp.concatenate(picks, axis=0)
    flags = jnp.broadcast_to(jnp.sum(picks, axis=1, keepdims=True), (picks.shape[0], LANES))
    return picks.astype(jnp.bfloat16), flags


def fetch_kernel(ids_ref, tokens_ref, held_ref, rows_ref, sems):
    features = tokens_ref.shape[1]
    parts = parts_of(features)
    copies = [
        pltpu.make_async_copy(tokens_ref.at[:, part], held_ref.at[:, part], sems.at[i])
        for i, part in enumerate(parts)
    ]
    for copy in copies:
        copy.start()
    picks, flags = picks_of(ids_ref, 2 * rows_ref.shape[0] // CAP)
    rows_ref[:, features:] = flags
    for copy, part in zip(copies, parts):
        copy.wait()
        rows_ref[:, part] = jnp.dot(
            picks, held_ref[:, part], preferred_element_type=jnp.float32
        )


def pair_kernel(
    other_ids_ref, rows_ref, mine_ref, other_ref, *out_refs, experts, peers, wanted, aligned
):
    out_refs, row_refs = out_refs[: -experts // 2], out_refs[-experts // 2 :]
    features = mine_ref.shape[1]
    e = lax.axis_index("expert")
    d = lax.axis_index("dp")

    picks, flags = picks_of(other_ids_ref, experts)

    def both(columns):
        return jnp.concatenate([mine_ref[:, columns], other_ref[:, columns]], axis=0)

    lead = both(slice(0, SBAND))

    def product(columns):
        return lax.dot_general(
            both(columns), lead, (((0,), (0,)), ((), ())), preferred_element_type=jnp.float32
        )

    if aligned:
        share = features // (experts * peers)
        half = LANES // 2
        window = share + half * (share // half % 2)
        for out_ref, pairs in zip(out_refs, wanted):
            for i, (m, k) in enumerate(pairs):
                start = ((e ^ m) * peers + (d ^ k)) * (share // half)
                odd = start % 2
                found = product(pl.ds(pl.multiple_of((start - odd) * half, LANES), window))
                if window > share:
                    found = jnp.where(odd == 1, found[half:], found[:share])
                out_ref[i * share : (i + 1) * share] = found
            filled = len(pairs) * share
            if out_ref.shape[0] > filled:
                out_ref[filled:] = jnp.zeros_like(out_ref[filled:])
    else:
        for part in parts_of(features):
            out_refs[0][part] = product(part)


    def put(columns, found):
        for i, ref in enumerate(row_refs):
            part = slice(i * CAP, (i + 1) * CAP)
            both_rows = jnp.concatenate([rows_ref[part, columns], found[part]], axis=0)
            ref[:, columns] = both_rows.astype(jnp.bfloat16)

    for part in parts_of(features):
        put(part, jnp.dot(picks, other_ref[:, part], preferred_element_type=jnp.float32))
    put(slice(features, features + LANES), flags)


def on_device(tokens, expert_ids):
    tok_rows, features = tokens.shape
    experts = lax.axis_size("expert")
    peers = lax.axis_size("dp")
    width = features // peers
    share = features // (experts * peers)
    anywhere = pl.BlockSpec(memory_space=pl.ANY)
    inside = pl.BlockSpec(memory_space=pltpu.VMEM)

    ids = expert_ids.T
    other = exchange(tokens, "dp", 1)
    other_ids = exchange(ids, "dp", 1)
    mine, own_rows = call(
        fetch_kernel,
        [
            jax.ShapeDtypeStruct(tokens.shape, tokens.dtype),
            jax.ShapeDtypeStruct((experts * CAP // 2, features + LANES), jnp.float32),
        ],
        ids,
        tokens,
        flops=0,
        nbytes=4 * tok_rows * features,
        in_specs=[inside, anywhere],
        out_specs=[inside, inside],
        scratch_shapes=[pltpu.SemaphoreType.DMA((len(parts_of(features)),))],
    )
    own_rows, mine, other, other_ids = lax.optimization_barrier(
        (own_rows, mine, other, other_ids)
    )

    even = range(0, peers, 2)
    far = range(2, experts, 2)
    groups = [[m + 1 for m in far], [*far], [1], [0]]
    wanted = [[(m, k) for m in group] for group in groups for k in even]
    aligned = share % (LANES // 2) == 0
    sizes = [len(pairs) * share for pairs in wanted]
    for i in range(1, peers // 2):
        sizes[i] += PAD
    found = call(
        functools.partial(
            pair_kernel, experts=experts, peers=peers, wanted=wanted, aligned=aligned
        ),
        [
            jax.ShapeDtypeStruct((size, SBAND), jnp.float32)
            for size in (sizes if aligned else [features])
        ]
        + [jax.ShapeDtypeStruct((2 * CAP, features + LANES), jnp.bfloat16)] * (experts // 2),
        other_ids,
        own_rows,
        mine,
        other,
        flops=4 * tok_rows * features * (SBAND + experts * CAP),
        nbytes=4 * tok_rows * features + 4 * features * SBAND,
    )
    blocks, outgoing = found[: -experts // 2], found[-experts // 2 :]
    if not aligned:
        e, d = lax.axis_index("expert"), lax.axis_index("dp")
        blocks = [
            jnp.concatenate(
                [
                    lax.dynamic_slice_in_dim(
                        blocks[0], ((e ^ m) * peers + (d ^ k)) * share, share, axis=0
                    )
                    for m, k in pairs
                ],
                axis=0,
            )
            for pairs in wanted
        ]
    def over_dp(i, after=None):
        own, *sent = blocks[i * (peers // 2) : (i + 1) * (peers // 2)]
        got = [exchange(tie(x, after), "dp", 2 * k + 2) for k, x in enumerate(sent)]
        return sum([x[: own.shape[0]] for x in got], own)

    odd = over_dp(0)
    near = exchange(odd, "expert", 1)
    paired = over_dp(1, odd) + near
    beside_sum = exchange(over_dp(2), "expert", 1)
    own = over_dp(3, near) + beside_sum

    arrived = [pass_on(outgoing[k], 2 * k) for k in range(experts // 2)]
    arrived[0] = jnp.where(lax.axis_index("dp") % 2 == 0, outgoing[0], arrived[0])

    rows = experts * CAP
    tail = BAND + LANES
    mine, give, *packed = call(
        functools.partial(split_kernel, peers=peers),
        [jax.ShapeDtypeStruct((rows, width + tail), jnp.bfloat16)] * 2
        + [jax.ShapeDtypeStruct((rows, 2 * width + tail), jnp.bfloat16)] * (peers // 2 - 1),
        *arrived,
        flops=0,
        nbytes=4 * rows * features,
    )
    across = [exchange(x, "dp", 2 * k + 2) for k, x in enumerate(packed)]
    beside = exchange(jnp.concatenate([give] + [x[:, width:] for x in across]), "dp", 1)
    gathered = [mine, *across, beside]
    paired = tie(paired, packed)
    others = [
        exchange(paired[i * share : (i + 1) * share], "expert", m) for i, m in enumerate(far)
    ]
    summed = sum(others, lax.optimization_barrier(own))
    shared_out = summed * (2.0 / (tok_rows * experts * peers))
    routed_out, shared_out = call(
        finish_kernel,
        [
            jax.ShapeDtypeStruct((1, BAND, width), jnp.float32),
            jax.ShapeDtypeStruct((share, SBAND), jnp.float32),
        ],
        *gathered,
        shared_out,
        flops=2 * BAND * width * rows * peers,
        nbytes=4 * BAND * width,
        in_specs=[inside] * (len(gathered) + 1),
        out_specs=[anywhere, anywhere],
        scratch_shapes=[
            pltpu.VMEM((BAND, width), jnp.float32),
            pltpu.SemaphoreType.DMA((BAND // LANES + 1,)),
        ],
    )
    return routed_out, shared_out


def solution(mesh):
    in_specs = (P(("groups", "expert", "dp"), None), P(("groups", "expert", "dp"), None))
    out_specs = (P(("groups", "expert"), None, "dp"), P(("groups", "expert", "dp"), None))
    return jax.shard_map(
        on_device, mesh=mesh, in_specs=in_specs, out_specs=out_specs, check_vma=False
    )
```
